32 devices in a mesh: row: 4 (over y, core), col: 8 (over z, x).
Axes of the slice: x: 2, y: 2, z: 4, core: 2. Of those that a mesh axis runs over, the one named last changes fastest.
Arguments:
- panel: float32 [6144, 2, 1024], P('row', None, 'col'), may hold values from -0.0625 to 0.0625
- solved: float32 [6144, 4096], P('row', 'col'), may hold values from -6 to 6
- rhs: float32 [2, 1024, 4096], P(None, 'row', 'col'), may hold values from -6 to 6
- coupling: float32 [1024, 1024], P('row'), may hold values from -0.1875 to 0.1875
- diag_inv: float32 [2, 1024, 1024], P(None, 'row'), as said below
- tile_row: int32 [4], replicated, may hold values from 0 to 3, as said below
- train_x: float32 [16, 2, 1024], P(None, None, 'row'), may hold values from -5 to 5
- train_task: int32 [2, 1024], P(None, 'row'), may hold values from 0 to 7
- cand_z: float32 [16, 512], P(None, 'col'), may hold values from -5 to 5
- cand_task: int32 [4096], P('col'), may hold values from 0 to 7
- inv_scale: float32 [16], replicated, may hold values from 0.15 to 0.35
- task_cov: float32 [8, 8], replicated, may hold values from 0.3 to 1.5
Outputs:
- adjoint: float32 [2, 1024, 4096], P(None, 'row', 'col')
- grad_z: float32 [16, 512], P(None, 'col')
- grad_cov: float32 [8, 8], replicated
The draws below stay inside these ranges and needn't reach their ends.
Inputs may be any that keep to these rules, and one draw needn't show every extreme that they name: `tile_row`: A permutation: each index of row holds exactly one tile of each block. Each diag_inv[k], its rows put in block order, is lower triangular with a positive diagonal.
All inputs are finite; a program needn't handle non-finite values.
Results may differ from the reference program's by a relative error of at most 0.0003.
Values sent between devices are 32-bit elements; how exact they have to be, the bound alone decides.
A program may use at most 64 MiB of HBM per device.

```python
import math
import jax
import jax.numpy as jnp
from jax import lax

BLOCK = 1024
TASKS = 8
DIM = 16
CAND = 512
ADJ = 4096
SOLVED = 6144
TILE = 256
N_ROW = 4


def row_ordering(key):
    return jax.random.permutation(jax.random.fold_in(key, 1009), N_ROW).astype(jnp.int32)


def draw_tile_row(key, part):
    return row_ordering(key)


def draw_diag_inv(key, part):
    ordering = row_ordering(key)
    key = jax.random.fold_in(key, 3)
    low_key, diag_key = jax.random.split(key)
    lower_part = jnp.clip(jax.random.normal(low_key, (2, BLOCK, BLOCK), jnp.float32), -3.0, 3.0)
    diagonal_vals = jax.random.uniform(diag_key, (2, BLOCK), jnp.float32, 0.6, 1.2)
    row_ids = jnp.arange(BLOCK)[:, None]
    col_ids = jnp.arange(BLOCK)[None, :]
    lower_part = jnp.where(row_ids > col_ids, lower_part / math.sqrt(BLOCK), 0.0)
    shaped_full = lower_part + diagonal_vals[:, :, None] * (row_ids == col_ids).astype(jnp.float32)
    shaped_full = shaped_full.reshape(2, N_ROW, TILE, BLOCK)
    return jnp.take(shaped_full, ordering, axis=1).reshape(2, BLOCK, BLOCK)


def place_ends(result, own_key, low, high):
    longest = result.shape.index(max(result.shape))
    spots = []
    for shift in (0, 1):
        where = [jax.random.randint(jax.random.fold_in(own_key, axis), (), 0, length) for axis, length in enumerate(result.shape)]
        where[longest] = (where[longest] + shift) % result.shape[longest]
        spots.append(tuple(where))
    return result.at[spots[0]].set(low).at[spots[1]].set(high)


def steps_of(own_key, extent, cuts, least, top_value):
    level, own = 1.0, jax.random.fold_in(own_key, 6)
    for axis_at, shards_of in cuts:
        draws = jnp.exp(jax.random.uniform(jax.random.fold_in(own, axis_at), (shards_of,), jnp.float32, least / len(cuts), top_value / len(cuts)))
        level = level * jnp.repeat(draws, extent[axis_at] // shards_of).reshape([-1 if axis == axis_at else 1 for axis in range(len(extent))])
    return level


def bell_draw(rng, dims, scale, most, shards=(), dtype=jnp.bfloat16):
    values = scale * jax.random.normal(rng, dims, jnp.float32)
    if shards:
        values = values * steps_of(rng, dims, shards, -0.22, 0.18)
    return jnp.clip(values, -most, most).astype(dtype)


def setup_inputs(seed: int = 0) -> dict:
    arg_keys = jax.random.split(jax.random.key(seed), 13)
    panel = bell_draw(arg_keys[0], (SOLVED, 2, BLOCK), (SOLVED + BLOCK) ** -0.5, 0.0625, ((0, 4), (2, 8)), jnp.float32)
    solved = bell_draw(arg_keys[1], (SOLVED, ADJ), 1.0, 6.0, ((0, 4), (1, 8)), jnp.float32)
    rhs = bell_draw(arg_keys[2], (2, BLOCK, ADJ), 1.0, 6.0, ((1, 4), (2, 8)), jnp.float32)
    coupling = bell_draw(arg_keys[3], (BLOCK, BLOCK), BLOCK ** -0.5, 0.1875, ((0, 4),), jnp.float32)
    diag_inv = draw_diag_inv(jax.random.fold_in(arg_keys[12], 71), 0)
    tile_row = draw_tile_row(jax.random.fold_in(arg_keys[12], 71), 0)
    train_x = bell_draw(arg_keys[6], (DIM, 2, BLOCK), 1.0, 5.0, ((2, 4),), jnp.float32)
    train_task = place_ends(jax.random.randint(arg_keys[7], (2, BLOCK), 0, TASKS), jax.random.fold_in(arg_keys[7], 1), 0, TASKS - 1).astype(jnp.int32)
    cand_z = bell_draw(arg_keys[8], (DIM, CAND), 1.0, 5.0, ((1, 8),), jnp.float32)
    cand_task = place_ends(jax.random.randint(arg_keys[9], (ADJ,), 0, TASKS), jax.random.fold_in(arg_keys[9], 1), 0, TASKS - 1).astype(jnp.int32)
    inv_scale = jnp.clip(jnp.exp(jax.random.uniform(arg_keys[10], (DIM,), jnp.float32, math.log(0.15), math.log(0.35))), 0.15, 0.35)
    task_cov = jnp.clip(jax.random.uniform(arg_keys[11], (TASKS, TASKS), jnp.float32, 0.3, 1.5), 0.3, 1.5)
    return dict(panel=panel, solved=solved, rhs=rhs, coupling=coupling, diag_inv=diag_inv, tile_row=tile_row, train_x=train_x, train_task=train_task, cand_z=cand_z, cand_task=cand_task, inv_scale=inv_scale, task_cov=task_cov)


PRECISE = lax.Precision.HIGHEST

def to_block(stored, ordering, block_axis):
    full_shape = stored.shape
    split_shape = full_shape[:block_axis] + (N_ROW, TILE) + full_shape[block_axis + 1:]
    return jnp.take(stored.reshape(split_shape), ordering, axis=block_axis).reshape(full_shape)

def reference(panel, solved, rhs, coupling, diag_inv, tile_row, train_x, train_task, cand_z, cand_task, inv_scale, task_cov):
    ordering = jnp.argsort(tile_row).astype(jnp.int32)
    rhs_block = to_block(rhs, ordering, 1)
    coupling_block = to_block(coupling, ordering, 0)
    inverse_block = to_block(diag_inv, ordering, 1)
    points = to_block(train_x, ordering, 2).reshape(DIM, 2 * BLOCK)
    point_task = to_block(train_task, ordering, 1).reshape(2 * BLOCK)
    update = jnp.einsum('skb,sa->kba', panel, solved, precision=PRECISE)
    late_block = jnp.dot(inverse_block[1].T, rhs_block[1] - update[1], precision=PRECISE)
    carried = update[0] + jnp.dot(coupling_block.T, late_block, precision=PRECISE)
    early_block = jnp.dot(inverse_block[0].T, rhs_block[0] - carried, precision=PRECISE)
    adjoint_block = jnp.stack([early_block, late_block])
    adjoint = to_block(adjoint_block, tile_row, 1)
    scaled_x = points * inv_scale[:, None]
    scaled_z = cand_z * inv_scale[:, None]
    distance = lax.optimization_barrier(jnp.sum(jnp.square(scaled_x[:, :, None] - scaled_z[:, None, :]), axis=0))
    kernel_vals = jnp.exp(-0.5 * distance)
    weighted = adjoint_block.reshape(2 * BLOCK, ADJ) * jnp.repeat(kernel_vals, TASKS, axis=1)
    point_onehot = (point_task[:, None] == jnp.arange(TASKS)[None, :]).astype(jnp.float32)
    query_onehot = (cand_task[:, None] == jnp.arange(TASKS)[None, :]).astype(jnp.float32)
    grad_cov = jnp.dot(jnp.dot(point_onehot.T, weighted, precision=PRECISE), query_onehot, precision=PRECISE) * (TASKS / math.sqrt(2 * BLOCK * ADJ))
    coupled_cov = jnp.dot(jnp.dot(point_onehot, task_cov, precision=PRECISE), query_onehot.T, precision=PRECISE)
    pulled = (weighted * coupled_cov).reshape(2 * BLOCK, CAND, TASKS).sum(axis=2)
    moment = jnp.dot(points, pulled, precision=PRECISE)
    totals = lax.optimization_barrier(jnp.sum(pulled, axis=0))
    grad_z = jnp.square(inv_scale)[:, None] * (moment - cand_z * totals[None, :]) * (16.0 / math.sqrt(2 * BLOCK))
    return (adjoint, grad_z, grad_cov)
```

```python
import math

import jax
import jax.numpy as jnp
from jax import lax
from jax.sharding import PartitionSpec as P

SPLIT = lax.Precision.HIGH


def tdot(left, right):
    return lax.dot_general(left, right, (((0,), (0,)), ((), ())), precision=SPLIT)


def dot(left, right):
    return jnp.dot(left, right, precision=SPLIT)


def per_device(
    panel,
    solved,
    rhs,
    coupling,
    diag_inv,
    tile_row,
    train_x,
    train_task,
    cand_z,
    cand_task,
    inv_scale,
    task_cov,
):
    row_count = lax.axis_size("row")
    col_count = lax.axis_size("col")
    outer_count = col_count // 2
    me_row = lax.axis_index("row")
    me_col = lax.axis_index("col")
    outer, inner = me_col // 2, me_col % 2
    tile_rows = rhs.shape[1]
    width = panel.shape[2]
    block_rows = tile_rows * row_count
    adj_width = solved.shape[1]
    task_count = task_cov.shape[0]

    swap = [(c, c ^ 1) for c in range(col_count)]
    ahead = [(c, c + 2) for c in range(col_count - 2)]
    back = [(c + 2, c) for c in range(col_count - 2)]

    def chain(block):
        if outer_count == 4:
            r1 = lax.ppermute(block, "col", ahead)
            l1 = lax.ppermute(block, "col", back)
            r2 = lax.ppermute(r1, "col", ahead)
            l2 = lax.ppermute(l1, "col", back)
            r3 = lax.ppermute(r2, "col", ahead)
            l3 = lax.ppermute(l2, "col", back)
            first = jnp.where(outer == 0, l1, r1)
            second = jnp.where(outer <= 1, l2, r2)
            third = jnp.where(outer == 0, l3, jnp.where(outer == 3, r3, l1))
            return [block, first, second, third]
        groups = [[o * 2 + i for o in range(outer_count)] for i in range(2)]
        whole = lax.all_gather(block, "col", axis_index_groups=groups, axis=1, tiled=True)
        return [whole]

    if outer_count == 4:
        sources = jnp.stack([
            outer,
            jnp.where(outer == 0, 1, outer - 1),
            jnp.where(outer <= 1, outer + 2, outer - 2),
            jnp.where(outer == 0, 3, jnp.where(outer == 3, 0, outer + 1)),
        ])
        pieces = jnp.stack([sources * 2 + inner, sources * 2 + 1 - inner], axis=1).reshape(-1)
    else:
        sources = jnp.arange(outer_count)
        pieces = jnp.concatenate([sources * 2 + inner, sources * 2 + 1 - inner])
    per_tile = tile_rows // width
    stored_of = jnp.argsort(tile_row)
    piece_at = stored_of[pieces // per_tile] * per_tile + pieces % per_tile
    relative = tile_row[me_row ^ jnp.arange(row_count)]

    def column_order(matrix):
        split = matrix.reshape(matrix.shape[0], row_count, tile_rows)
        return jnp.take(split, relative, axis=1).reshape(matrix.shape)

    def scatter_rows(partial_value):
        kept = partial_value.reshape(row_count, tile_rows, adj_width)
        bit = 1
        while bit < row_count:
            split = kept.reshape(kept.shape[0] // 2, 2, tile_rows, adj_width)
            perm = [(r, r ^ bit) for r in range(row_count)]
            kept = split[:, 0] + lax.ppermute(split[:, 1], "row", perm)
            bit *= 2
        return kept[0]

    panel_late = panel[:, 1, :]
    panel_early = panel[:, 0, :]
    other_solved = lax.ppermute(solved, "col", swap)
    late_blocks = chain(panel_late)
    early_blocks = chain(panel_early)
    inverse_stored = lax.all_gather(diag_inv, "row", axis=1, tiled=True)

    def inverse_rows(index):
        split = inverse_stored[index].reshape(-1, width, block_rows)
        return column_order(jnp.take(split, piece_at, axis=0).reshape(block_rows, block_rows))

    def applied(blocks, inverse):
        total, start = None, 0
        for block in blocks:
            rows = 2 * block.shape[1]
            sent = tdot(block, other_solved)
            update = jnp.concatenate([tdot(block, solved), lax.ppermute(sent, "col", swap)])
            term = tdot(inverse[start : start + rows], update)
            total = term if total is None else total + term
            start += rows
        return total

    own_late = tdot(column_order(diag_inv[1]), rhs[1])
    late_block = scatter_rows(own_late - applied(late_blocks, inverse_rows(1)))
    inverse_early = inverse_rows(0)
    stored_early = inverse_stored[0].reshape(row_count, tile_rows, block_rows)
    block_early = jnp.take(stored_early, stored_of, axis=0).reshape(block_rows, block_rows)
    carried = column_order(dot(coupling, block_early))
    own_early = tdot(column_order(diag_inv[0]), rhs[0]) - tdot(carried, late_block)
    early_block = scatter_rows(own_early - applied(early_blocks, inverse_early))
    adjoint = jnp.stack([early_block, late_block])

    scaled_z = jnp.repeat(cand_z * inv_scale[:, None], task_count, axis=1)
    query_onehot = (cand_task[:, None] == jnp.arange(task_count)[None, :]).astype(jnp.float32)
    group = jnp.arange(adj_width)[:, None] // task_count == jnp.arange(cand_z.shape[1])[None, :]
    group = group.astype(jnp.float32)
    cov_rows = dot(task_cov, query_onehot.T)

    def gradients(index, block):
        points = train_x[:, index, :]
        scaled_x = points * inv_scale[:, None]
        distance = jnp.sum(jnp.square(scaled_x[:, :, None] - scaled_z[:, None, :]), axis=0)
        kernel_vals = jnp.exp(-0.5 * distance)
        task = train_task[index]
        point_onehot = (jnp.arange(task_count)[:, None] == task[None, :]).astype(jnp.float32)
        weighted = block * kernel_vals
        pulled = weighted * tdot(point_onehot, cov_rows)
        by_task = dot(point_onehot, weighted)
        moments = dot(jnp.concatenate([points, jnp.ones_like(points[:1])]), pulled)
        return by_task, moments

    late_task, late_moment = gradients(1, late_block)
    early_task, early_moment = gradients(0, early_block)
    cov_part = dot(late_task + early_task, query_onehot)
    moments = lax.psum(dot(late_moment + early_moment, group), "row")
    cov_total = lax.psum(cov_part, ("row", "col"))
    moment, totals = moments[:-1], moments[-1]
    grad_cov = cov_total * (task_count / math.sqrt(2 * block_rows * adj_width * col_count))
    grad_z = (
        jnp.square(inv_scale)[:, None]
        * (moment - cand_z * totals[None, :])
        * (16.0 / math.sqrt(2 * block_rows))
    )
    return (adjoint, grad_z, grad_cov)


def solution(mesh):
    placed = (
        P("row", None, "col"),
        P("row", "col"),
        P(None, "row", "col"),
        P("row", None),
        P(None, "row", None),
        P(),
        P(None, None, "row"),
        P(None, "row"),
        P(None, "col"),
        P("col"),
        P(),
        P(),
    )
    return jax.shard_map(
        per_device,
        mesh=mesh,
        in_specs=placed,
        out_specs=(P(None, "row", "col"), P(None, "col"), P()),
        check_vma=False,
    )
```

```python
import functools
import math

import jax
import jax.numpy as jnp
from jax import lax
from jax.experimental import pallas as pl
from jax.experimental.pallas import tpu as pltpu
from jax.sharding import PartitionSpec as P

SPLIT = lax.Precision.HIGH
MESH = pl.DeviceIdType.MESH


def tdot(left, right):
    return lax.dot_general(left, right, (((0,), (0,)), ((), ())), precision=SPLIT)


def dot(left, right):
    return jnp.dot(left, right, precision=SPLIT)


def sums_kernel(row_count, col_count, top, x_ref, out_ref, rbuf, cbuf, rsend, rrecv, csend, crecv):
    me_row, me_col = lax.axis_index("row"), lax.axis_index("col")
    barrier = pltpu.get_barrier_semaphore()
    for j in range(1, row_count):
        pl.semaphore_signal(barrier, inc=1, device_id={"row": me_row ^ j}, device_id_type=MESH)
    for j in range(1, col_count):
        pl.semaphore_signal(barrier, inc=1, device_id={"col": me_col ^ j}, device_id_type=MESH)
    pl.semaphore_wait(barrier, row_count + col_count - 2)

    def exchange(axis, me, count, source, buffer, send, recv):
        copies = []
        for j in range(1, count):
            copy = pltpu.make_async_remote_copy(
                src_ref=source,
                dst_ref=buffer.at[me],
                send_sem=send.at[j],
                recv_sem=recv.at[j],
                device_id={axis: me ^ j},
                device_id_type=MESH,
            )
            copy.start()
            copies.append(copy)
        buffer[me] = source[...]
        for copy in copies:
            copy.wait()
        total = buffer[0]
        for j in range(1, count):
            total = total + buffer[j]
        return total

    out_ref[...] = exchange("row", me_row, row_count, x_ref, rbuf, rsend, rrecv)
    cov = out_ref.at[pl.ds(top, 8)]
    out_ref[pl.ds(top, 8)] = exchange("col", me_col, col_count, cov, cbuf, csend, crecv)


def small_sums(moments, cov_part, row_count, col_count):
    rows, wide = moments.shape
    tasks = cov_part.shape[0]
    top = -(-rows // 8) * 8
    packed = jnp.zeros((top + 8, 128), jnp.float32)
    packed = packed.at[:rows, :wide].set(moments).at[top : top + tasks, :tasks].set(cov_part)
    out = pl.pallas_call(
        functools.partial(sums_kernel, row_count, col_count, top),
        out_shape=jax.ShapeDtypeStruct(packed.shape, jnp.float32),
        in_specs=[pl.BlockSpec(memory_space=pltpu.VMEM)],
        out_specs=pl.BlockSpec(memory_space=pltpu.VMEM),
        scratch_shapes=[
            pltpu.VMEM((row_count,) + packed.shape, jnp.float32),
            pltpu.VMEM((col_count, 8, 128), jnp.float32),
            pltpu.SemaphoreType.DMA((row_count,)),
            pltpu.SemaphoreType.DMA((row_count,)),
            pltpu.SemaphoreType.DMA((col_count,)),
            pltpu.SemaphoreType.DMA((col_count,)),
        ],
        compiler_params=pltpu.CompilerParams(collective_id=0, has_side_effects=True),
    )(packed)
    return out[:rows, :wide], out[top : top + tasks, :tasks]


def per_device(
    panel,
    solved,
    rhs,
    coupling,
    diag_inv,
    tile_row,
    train_x,
    train_task,
    cand_z,
    cand_task,
    inv_scale,
    task_cov,
):
    row_count = lax.axis_size("row")
    col_count = lax.axis_size("col")
    outer_count = col_count // 2
    me_row = lax.axis_index("row")
    me_col = lax.axis_index("col")
    outer, inner = me_col // 2, me_col % 2
    tile_rows = rhs.shape[1]
    width = panel.shape[2]
    block_rows = tile_rows * row_count
    adj_width = solved.shape[1]
    task_count = task_cov.shape[0]

    swap = [(c, c ^ 1) for c in range(col_count)]
    ahead = [(c, c + 2) for c in range(col_count - 2)]
    back = [(c + 2, c) for c in range(col_count - 2)]

    def hop(pair):
        return lax.ppermute(pair[0], "col", ahead), lax.ppermute(pair[1], "col", back)

    def after(value, *others):
        return lax.optimization_barrier((value,) + others)[0]

    def slots(block, one, two, three):
        (r1, l1), (r2, l2), (r3, l3) = one, two, three
        first = jnp.where(outer == 0, l1, r1)
        second = jnp.where(outer <= 1, l2, r2)
        third = jnp.where(outer == 0, l3, jnp.where(outer == 3, r3, l1))
        return [block, first, second, third]

    def whole(block):
        groups = [[o * 2 + i for o in range(outer_count)] for i in range(2)]
        return lax.all_gather(block, "col", axis_index_groups=groups, axis=1, tiled=True)

    per_tile = tile_rows // width
    stored_of = jnp.argsort(tile_row)
    chained = outer_count == 4 and per_tile == 2

    panel_late = panel[:, 1, :]
    panel_early = panel[:, 0, :]
    other_solved = lax.ppermute(solved, "col", swap)
    if chained:
        late1 = hop((panel_late, panel_late))
        start = after(panel_early, *late1)
        early1 = hop((start, start))
        late2 = hop(late1)
        late3 = hop(late2)
        early2 = hop(early1)
        early3 = hop(early2)
        late_slots = slots(panel_late, late1, late2, late3)
        early_slots = slots(panel_early, early1, early2, early3)
        sources = [
            outer,
            jnp.where(outer == 0, 1, outer - 1),
            jnp.where(outer <= 1, outer + 2, outer - 2),
            jnp.where(outer == 0, 3, jnp.where(outer == 3, 0, outer + 1)),
        ]
    else:
        late_slots, early_slots = [whole(panel_late)], [whole(panel_early)]
    inverse_stored = lax.all_gather(diag_inv, "row", axis=1, tiled=True)

    def rows_of(matrix, tile):
        return lax.dynamic_slice_in_dim(matrix, tile * tile_rows, tile_rows, axis=0)

    def swapped(block):
        return tdot(block, solved), lax.ppermute(tdot(block, other_solved), "col", swap)

    def applied(blocks, inverse, total):
        if chained:
            for block, source in zip(blocks, sources):
                own, got = swapped(block)
                update = jnp.concatenate(
                    [jnp.where(inner == 0, own, got), jnp.where(inner == 0, got, own)]
                )
                total = total - tdot(rows_of(inverse, stored_of[source]), update)
            return total
        own, got = swapped(blocks[0])
        ids = jnp.arange(outer_count) * 2
        pieces = jnp.concatenate([ids + inner, ids + 1 - inner])
        position = stored_of[pieces // per_tile] * per_tile + pieces % per_tile
        update = jnp.concatenate([own, got]).reshape(-1, width, adj_width)
        update = jnp.take(update, jnp.argsort(position), axis=0, mode="clip")
        return total - tdot(inverse, update.reshape(block_rows, adj_width))

    def scatter_rows(partial_value):
        done = []
        cut = 2 if adj_width % 256 == 0 else 1
        for part in jnp.split(partial_value, cut, axis=1):
            kept = [rows_of(part, tile_row[me_row ^ j]) for j in range(row_count)]
            bit = 1
            while bit < row_count:
                perm = [(r, r ^ bit) for r in range(row_count)]
                got = lax.ppermute(jnp.concatenate(kept[1::2]), "row", perm)
                kept = [
                    mine + got[at * tile_rows : (at + 1) * tile_rows]
                    for at, mine in enumerate(kept[0::2])
                ]
                bit *= 2
            done.append(kept[0])
        return jnp.concatenate(done, axis=1)

    late_block = scatter_rows(applied(late_slots, inverse_stored[1], tdot(diag_inv[1], rhs[1])))
    carried = sum(
        dot(
            lax.dynamic_slice_in_dim(coupling, tile_row[r] * tile_rows, tile_rows, axis=1),
            inverse_stored[0, r * tile_rows : (r + 1) * tile_rows],
        )
        for r in range(row_count)
    )
    own_early = tdot(diag_inv[0], rhs[0]) - tdot(carried, late_block)
    early_block = scatter_rows(applied(early_slots, inverse_stored[0], own_early))
    adjoint = jnp.stack([early_block, late_block])

    scaled_z = jnp.repeat(cand_z * inv_scale[:, None], task_count, axis=1)
    query_onehot = (cand_task[:, None] == jnp.arange(task_count)[None, :]).astype(jnp.float32)
    group = jnp.arange(adj_width)[:, None] // task_count == jnp.arange(cand_z.shape[1])[None, :]
    group = group.astype(jnp.float32)
    cov_rows = dot(task_cov, query_onehot.T)

    def gradients(index, block):
        points = train_x[:, index, :]
        scaled_x = points * inv_scale[:, None]
        distance = jnp.sum(jnp.square(scaled_x[:, :, None] - scaled_z[:, None, :]), axis=0)
        kernel_vals = jnp.exp(-0.5 * distance)
        task = train_task[index]
        point_onehot = (jnp.arange(task_count)[:, None] == task[None, :]).astype(jnp.float32)
        weighted = block * kernel_vals
        pulled = weighted * tdot(point_onehot, cov_rows)
        by_task = dot(point_onehot, weighted)
        moments = dot(jnp.concatenate([points, jnp.ones_like(points[:1])]), pulled)
        return by_task, moments

    late_task, late_moment = gradients(1, late_block)
    early_task, early_moment = gradients(0, early_block)
    cov_part = dot(late_task + early_task, query_onehot)
    moments = dot(late_moment + early_moment, group)
    moments, cov_total = small_sums(moments, cov_part, row_count, col_count)
    moment, totals = moments[:-1], moments[-1]
    grad_cov = cov_total * (task_count / math.sqrt(2 * block_rows * adj_width * col_count))
    grad_z = (
        jnp.square(inv_scale)[:, None]
        * (moment - cand_z * totals[None, :])
        * (16.0 / math.sqrt(2 * block_rows))
    )
    return (adjoint, grad_z, grad_cov)


def solution(mesh):
    placed = (
        P("row", None, "col"),
        P("row", "col"),
        P(None, "row", "col"),
        P("row", None),
        P(None, "row", None),
        P(),
        P(None, None, "row"),
        P(None, "row"),
        P(None, "col"),
        P("col"),
        P(),
        P(),
    )
    return jax.shard_map(
        per_device,
        mesh=mesh,
        in_specs=placed,
        out_specs=(P(None, "row", "col"), P(None, "col"), P()),
        check_vma=False,
    )
```

```python
import functools
import math

import jax
import jax.numpy as jnp
from jax import lax
from jax.experimental import pallas as pl
from jax.experimental.pallas import tpu as pltpu
from jax.sharding import PartitionSpec as P

SPLIT = lax.Precision.HIGH
MESH = pl.DeviceIdType.MESH


def tdot(left, right):
    return lax.dot_general(left, right, (((0,), (0,)), ((), ())), precision=SPLIT)


def halves(value):
    high = lax.reduce_precision(value, 8, 7)
    return jnp.concatenate(
        [high.astype(jnp.bfloat16), (value - high).astype(jnp.bfloat16)], axis=1
    )


def halves_tdot(left, right):
    both = lax.dot_general(
        left, right, (((0,), (0,)), ((), ())), preferred_element_type=jnp.float32
    )
    rows, columns = left.shape[1] // 2, right.shape[1] // 2
    cross = both[rows:, :columns] + both[:rows, columns:]
    return both[:rows, :columns] + cross


def dot(left, right):
    return jnp.dot(left, right, precision=SPLIT)


def sums_kernel(row_count, col_count, top, x_ref, out_ref, rbuf, cbuf, rsend, rrecv, csend, crecv):
    me_row, me_col = lax.axis_index("row"), lax.axis_index("col")
    barrier = pltpu.get_barrier_semaphore()
    for j in range(1, row_count):
        pl.semaphore_signal(barrier, inc=1, device_id={"row": me_row ^ j}, device_id_type=MESH)
    for j in range(1, col_count):
        pl.semaphore_signal(barrier, inc=1, device_id={"col": me_col ^ j}, device_id_type=MESH)
    pl.semaphore_wait(barrier, row_count + col_count - 2)

    def exchange(axis, me, count, source, buffer, send, recv):
        copies = []
        for j in range(1, count):
            copy = pltpu.make_async_remote_copy(
                src_ref=source,
                dst_ref=buffer.at[me],
                send_sem=send.at[j],
                recv_sem=recv.at[j],
                device_id={axis: me ^ j},
                device_id_type=MESH,
            )
            copy.start()
            copies.append(copy)
        buffer[me] = source[...]
        for copy in copies:
            copy.wait()
        total = buffer[0]
        for j in range(1, count):
            total = total + buffer[j]
        return total

    out_ref[...] = exchange("row", me_row, row_count, x_ref, rbuf, rsend, rrecv)
    cov = out_ref.at[pl.ds(top, 8)]
    out_ref[pl.ds(top, 8)] = exchange("col", me_col, col_count, cov, cbuf, csend, crecv)


def small_sums(moments, cov_part, row_count, col_count):
    rows, wide = moments.shape
    tasks = cov_part.shape[0]
    top = -(-rows // 8) * 8
    packed = jnp.zeros((top + 8, 128), jnp.float32)
    packed = packed.at[:rows, :wide].set(moments).at[top : top + tasks, :tasks].set(cov_part)
    out = pl.pallas_call(
        functools.partial(sums_kernel, row_count, col_count, top),
        out_shape=jax.ShapeDtypeStruct(packed.shape, jnp.float32),
        in_specs=[pl.BlockSpec(memory_space=pltpu.VMEM)],
        out_specs=pl.BlockSpec(memory_space=pltpu.VMEM),
        scratch_shapes=[
            pltpu.VMEM((row_count,) + packed.shape, jnp.float32),
            pltpu.VMEM((col_count, 8, 128), jnp.float32),
            pltpu.SemaphoreType.DMA((row_count,)),
            pltpu.SemaphoreType.DMA((row_count,)),
            pltpu.SemaphoreType.DMA((col_count,)),
            pltpu.SemaphoreType.DMA((col_count,)),
        ],
        compiler_params=pltpu.CompilerParams(collective_id=0, has_side_effects=True),
    )(packed)
    return out[:rows, :wide], out[top : top + tasks, :tasks]


def per_device(
    panel,
    solved,
    rhs,
    coupling,
    diag_inv,
    tile_row,
    train_x,
    train_task,
    cand_z,
    cand_task,
    inv_scale,
    task_cov,
):
    row_count = lax.axis_size("row")
    col_count = lax.axis_size("col")
    outer_count = col_count // 2
    me_row = lax.axis_index("row")
    me_col = lax.axis_index("col")
    outer, inner = me_col // 2, me_col % 2
    tile_rows = rhs.shape[1]
    width = panel.shape[2]
    block_rows = tile_rows * row_count
    adj_width = solved.shape[1]
    task_count = task_cov.shape[0]

    swap = [(c, c ^ 1) for c in range(col_count)]
    ahead = [(c, c + 2) for c in range(col_count - 2)]
    back = [(c + 2, c) for c in range(col_count - 2)]

    def hop(pair):
        return lax.ppermute(pair[0], "col", ahead), lax.ppermute(pair[1], "col", back)

    def after(value, *others):
        return lax.optimization_barrier((value,) + others)[0]

    def slots(block, one, two, three):
        (r1, l1), (r2, l2), (r3, l3) = one, two, three
        first = jnp.where(outer == 0, l1, r1)
        second = jnp.where(outer <= 1, l2, r2)
        third = jnp.where(outer == 0, l3, jnp.where(outer == 3, r3, l1))
        return [block, first, second, third]

    def whole(block):
        groups = [[o * 2 + i for o in range(outer_count)] for i in range(2)]
        return lax.all_gather(block, "col", axis_index_groups=groups, axis=1, tiled=True)

    per_tile = tile_rows // width
    stored_of = jnp.argsort(tile_row)
    chained = outer_count == 4 and per_tile == 2

    panel_late = panel[:, 1, :]
    panel_early = panel[:, 0, :]
    other_solved = lax.ppermute(solved, "col", swap)
    if chained:
        late1 = hop((panel_late, panel_late))
        early1 = hop((panel_early, panel_early))
        late2 = hop(late1)
        early2 = hop(early1)
        late3 = hop(late2)
        early3 = hop(early2)
        late_slots = slots(panel_late, late1, late2, late3)
        early_slots = slots(panel_early, early1, early2, early3)
        sources = [
            outer,
            jnp.where(outer == 0, 1, outer - 1),
            jnp.where(outer <= 1, outer + 2, outer - 2),
            jnp.where(outer == 0, 3, jnp.where(outer == 3, 0, outer + 1)),
        ]
    else:
        late_slots, early_slots = [whole(panel_late)], [whole(panel_early)]
    inverse_early = lax.all_gather(diag_inv[0], "row", axis=0, tiled=True)
    inverse_late = lax.all_gather(
        after(diag_inv[1], inverse_early), "row", axis=0, tiled=True
    )
    own_halves, other_halves = halves(solved), halves(other_solved)

    def rows_of(matrix, tile):
        return lax.dynamic_slice_in_dim(matrix, tile * tile_rows, tile_rows, axis=0)

    def swapped(block):
        parts = halves(block)
        sent = halves_tdot(parts, other_halves)
        return halves_tdot(parts, own_halves), lax.ppermute(sent, "col", swap)

    def applied(blocks, inverse, total):
        if chained:
            for block, source in zip(blocks, sources):
                own, got = swapped(block)
                update = jnp.concatenate(
                    [jnp.where(inner == 0, own, got), jnp.where(inner == 0, got, own)]
                )
                total = total - tdot(rows_of(inverse, stored_of[source]), update)
            return total
        own, got = swapped(blocks[0])
        ids = jnp.arange(outer_count) * 2
        pieces = jnp.concatenate([ids + inner, ids + 1 - inner])
        position = stored_of[pieces // per_tile] * per_tile + pieces % per_tile
        update = jnp.concatenate([own, got]).reshape(-1, width, adj_width)
        update = jnp.take(update, jnp.argsort(position), axis=0, mode="clip")
        return total - tdot(inverse, update.reshape(block_rows, adj_width))

    def scatter_rows(partial_value):
        done = []
        cut = 2 if adj_width % 256 == 0 else 1
        for part in jnp.split(partial_value, cut, axis=1):
            kept = [rows_of(part, tile_row[me_row ^ j]) for j in range(row_count)]
            bit = 1
            while bit < row_count:
                perm = [(r, r ^ bit) for r in range(row_count)]
                got = lax.ppermute(jnp.concatenate(kept[1::2]), "row", perm)
                kept = [
                    mine + got[at * tile_rows : (at + 1) * tile_rows]
                    for at, mine in enumerate(kept[0::2])
                ]
                bit *= 2
            done.append(kept[0])
        return jnp.concatenate(done, axis=1)

    late_part = applied(late_slots, inverse_late, tdot(diag_inv[1], rhs[1]))
    late_block = scatter_rows(late_part)
    carried = sum(
        dot(
            lax.dynamic_slice_in_dim(coupling, tile_row[r] * tile_rows, tile_rows, axis=1),
            inverse_early[r * tile_rows : (r + 1) * tile_rows],
        )
        for r in range(row_count)
    )
    carried = lax.all_gather(carried, "row", axis=0, tiled=False)
    carried = jnp.take(carried, stored_of, axis=0, mode="clip").reshape(block_rows, block_rows)
    own_early = tdot(diag_inv[0], rhs[0]) - tdot(carried, late_part)
    early_block = scatter_rows(applied(early_slots, inverse_early, own_early))
    adjoint = jnp.stack([early_block, late_block])

    scaled_z = jnp.repeat(cand_z * inv_scale[:, None], task_count, axis=1)
    query_onehot = (cand_task[:, None] == jnp.arange(task_count)[None, :]).astype(jnp.float32)
    group = jnp.arange(adj_width)[:, None] // task_count == jnp.arange(cand_z.shape[1])[None, :]
    group = group.astype(jnp.float32)
    cov_rows = dot(task_cov, query_onehot.T)

    def gradients(index, block):
        points = train_x[:, index, :]
        scaled_x = points * inv_scale[:, None]
        distance = jnp.sum(jnp.square(scaled_x[:, :, None] - scaled_z[:, None, :]), axis=0)
        kernel_vals = jnp.exp(-0.5 * distance)
        task = train_task[index]
        point_onehot = (jnp.arange(task_count)[:, None] == task[None, :]).astype(jnp.float32)
        weighted = block * kernel_vals
        pulled = weighted * tdot(point_onehot, cov_rows)
        by_task = dot(point_onehot, weighted)
        moments = dot(jnp.concatenate([points, jnp.ones_like(points[:1])]), pulled)
        return by_task, moments

    late_task, late_moment = gradients(1, late_block)
    early_task, early_moment = gradients(0, early_block)
    cov_part = dot(late_task + early_task, query_onehot)
    moments = dot(late_moment + early_moment, group)
    moments, cov_total = small_sums(moments, cov_part, row_count, col_count)
    moment, totals = moments[:-1], moments[-1]
    grad_cov = cov_total * (task_count / math.sqrt(2 * block_rows * adj_width * col_count))
    grad_z = (
        jnp.square(inv_scale)[:, None]
        * (moment - cand_z * totals[None, :])
        * (16.0 / math.sqrt(2 * block_rows))
    )
    return (adjoint, grad_z, grad_cov)


def solution(mesh):
    placed = (
        P("row", None, "col"),
        P("row", "col"),
        P(None, "row", "col"),
        P("row", None),
        P(None, "row", None),
        P(),
        P(None, None, "row"),
        P(None, "row"),
        P(None, "col"),
        P("col"),
        P(),
        P(),
    )
    return jax.shard_map(
        per_device,
        mesh=mesh,
        in_specs=placed,
        out_specs=(P(None, "row", "col"), P(None, "col"), P()),
        check_vma=False,
    )
```

```python
import functools
import math

import jax
import jax.numpy as jnp
from jax import lax
from jax.experimental import pallas as pl
from jax.experimental.pallas import tpu as pltpu
from jax.sharding import PartitionSpec as P

SPLIT = lax.Precision.HIGH
MESH = pl.DeviceIdType.MESH


def tdot(left, right):
    return lax.dot_general(left, right, (((0,), (0,)), ((), ())), precision=SPLIT)


def halves(value):
    high = lax.reduce_precision(value, 8, 7)
    return jnp.concatenate(
        [high.astype(jnp.bfloat16), (value - high).astype(jnp.bfloat16)], axis=1
    )


def halves_tdot(left, right):
    both = lax.dot_general(
        left, right, (((0,), (0,)), ((), ())), preferred_element_type=jnp.float32
    )
    rows, columns = left.shape[1] // 2, right.shape[1] // 2
    cross = both[rows:, :columns] + both[:rows, columns:]
    return both[:rows, :columns] + cross


def dot(left, right):
    return jnp.dot(left, right, precision=SPLIT)


def sums_kernel(row_count, col_count, top, x_ref, out_ref, rbuf, cbuf, rsend, rrecv, csend, crecv):
    me_row, me_col = lax.axis_index("row"), lax.axis_index("col")
    barrier = pltpu.get_barrier_semaphore()
    for j in range(1, row_count):
        pl.semaphore_signal(barrier, inc=1, device_id={"row": me_row ^ j}, device_id_type=MESH)
    for j in range(1, col_count):
        pl.semaphore_signal(barrier, inc=1, device_id={"col": me_col ^ j}, device_id_type=MESH)
    pl.semaphore_wait(barrier, row_count + col_count - 2)

    def exchange(axis, me, count, source, buffer, send, recv):
        copies = []
        for j in range(1, count):
            copy = pltpu.make_async_remote_copy(
                src_ref=source,
                dst_ref=buffer.at[me],
                send_sem=send.at[j],
                recv_sem=recv.at[j],
                device_id={axis: me ^ j},
                device_id_type=MESH,
            )
            copy.start()
            copies.append(copy)
        buffer[me] = source[...]
        for copy in copies:
            copy.wait()
        total = buffer[0]
        for j in range(1, count):
            total = total + buffer[j]
        return total

    out_ref[...] = exchange("row", me_row, row_count, x_ref, rbuf, rsend, rrecv)
    cov = out_ref.at[pl.ds(top, 8)]
    out_ref[pl.ds(top, 8)] = exchange("col", me_col, col_count, cov, cbuf, csend, crecv)


def small_sums(moments, cov_part, row_count, col_count):
    rows, wide = moments.shape
    tasks = cov_part.shape[0]
    top = -(-rows // 8) * 8
    packed = jnp.zeros((top + 8, 128), jnp.float32)
    packed = packed.at[:rows, :wide].set(moments).at[top : top + tasks, :tasks].set(cov_part)
    out = pl.pallas_call(
        functools.partial(sums_kernel, row_count, col_count, top),
        out_shape=jax.ShapeDtypeStruct(packed.shape, jnp.float32),
        in_specs=[pl.BlockSpec(memory_space=pltpu.VMEM)],
        out_specs=pl.BlockSpec(memory_space=pltpu.VMEM),
        scratch_shapes=[
            pltpu.VMEM((row_count,) + packed.shape, jnp.float32),
            pltpu.VMEM((col_count, 8, 128), jnp.float32),
            pltpu.SemaphoreType.DMA((row_count,)),
            pltpu.SemaphoreType.DMA((row_count,)),
            pltpu.SemaphoreType.DMA((col_count,)),
            pltpu.SemaphoreType.DMA((col_count,)),
        ],
        compiler_params=pltpu.CompilerParams(collective_id=0, has_side_effects=True),
    )(packed)
    return out[:rows, :wide], out[top : top + tasks, :tasks]


def per_device(
    panel,
    solved,
    rhs,
    coupling,
    diag_inv,
    tile_row,
    train_x,
    train_task,
    cand_z,
    cand_task,
    inv_scale,
    task_cov,
):
    row_count = lax.axis_size("row")
    col_count = lax.axis_size("col")
    outer_count = col_count // 2
    me_row = lax.axis_index("row")
    me_col = lax.axis_index("col")
    outer, inner = me_col // 2, me_col % 2
    tile_rows = rhs.shape[1]
    width = panel.shape[2]
    block_rows = tile_rows * row_count
    adj_width = solved.shape[1]
    task_count = task_cov.shape[0]

    swap = [(c, c ^ 1) for c in range(col_count)]
    ahead = [(c, c + 2) for c in range(col_count - 2)]
    back = [(c + 2, c) for c in range(col_count - 2)]

    def hop(pair):
        return lax.ppermute(pair[0], "col", ahead), lax.ppermute(pair[1], "col", back)

    def after(value, *others):
        return lax.optimization_barrier((value,) + others)[0]

    def slots(block, one, two, three):
        (r1, l1), (r2, l2), (r3, l3) = one, two, three
        first = jnp.where(outer == 0, l1, r1)
        second = jnp.where(outer <= 1, l2, r2)
        third = jnp.where(outer == 0, l3, jnp.where(outer == 3, r3, l1))
        return [block, first, second, third]

    def whole(block):
        groups = [[o * 2 + i for o in range(outer_count)] for i in range(2)]
        return lax.all_gather(block, "col", axis_index_groups=groups, axis=1, tiled=True)

    per_tile = tile_rows // width
    stored_of = jnp.argsort(tile_row)
    chained = outer_count == 4 and per_tile == 2

    panel_late = panel[:, 1, :]
    panel_early = panel[:, 0, :]
    other_solved = lax.ppermute(solved, "col", swap)
    if chained:
        late1 = hop((panel_late, panel_late))
        early1 = hop((panel_early, panel_early))
        late2 = hop(late1)
        early2 = hop(early1)
        late3 = hop(late2)
        early2 = lax.optimization_barrier(early2 + (other_solved,))[:2]
        early3 = hop(early2)
        late_slots = slots(panel_late, late1, late2, late3)
        early_slots = slots(panel_early, early1, early2, early3)
        sources = [
            outer,
            jnp.where(outer == 0, 1, outer - 1),
            jnp.where(outer <= 1, outer + 2, outer - 2),
            jnp.where(outer == 0, 3, jnp.where(outer == 3, 0, outer + 1)),
        ]
    else:
        late_slots, early_slots = [whole(panel_late)], [whole(panel_early)]
    inverse_early = lax.all_gather(diag_inv[0], "row", axis=0, tiled=True)
    inverse_late = lax.all_gather(
        after(diag_inv[1], inverse_early), "row", axis=0, tiled=True
    )
    own_halves, other_halves = halves(solved), halves(other_solved)

    def rows_of(matrix, tile):
        return lax.dynamic_slice_in_dim(matrix, tile * tile_rows, tile_rows, axis=0)

    def swapped(block):
        parts = halves(block)
        sent = halves_tdot(parts, other_halves)
        return halves_tdot(parts, own_halves), lax.ppermute(sent, "col", swap)

    def applied(blocks, inverse, total, before=(), beside=()):
        if chained:
            for at, (block, source) in enumerate(zip(blocks, sources)):
                if at == len(blocks) - 1:
                    block, total = lax.optimization_barrier((block, total) + before)[:2]
                own, got = swapped(block)
                if at == len(blocks) - 1:
                    got = after(got, *beside)
                update = jnp.concatenate(
                    [jnp.where(inner == 0, own, got), jnp.where(inner == 0, got, own)]
                )
                total = total - tdot(rows_of(inverse, stored_of[source]), update)
            return total
        own, got = swapped(blocks[0])
        ids = jnp.arange(outer_count) * 2
        pieces = jnp.concatenate([ids + inner, ids + 1 - inner])
        position = stored_of[pieces // per_tile] * per_tile + pieces % per_tile
        update = jnp.concatenate([own, got]).reshape(-1, width, adj_width)
        update = jnp.take(update, jnp.argsort(position), axis=0, mode="clip")
        return total - tdot(inverse, update.reshape(block_rows, adj_width))

    def scatter_rows(partial_value):
        done, first = [], []
        cut = 2 if adj_width % 256 == 0 else 1
        for part in jnp.split(partial_value, cut, axis=1):
            kept = [rows_of(part, tile_row[me_row ^ j]) for j in range(row_count)]
            bit = 1
            while bit < row_count:
                perm = [(r, r ^ bit) for r in range(row_count)]
                got = lax.ppermute(jnp.concatenate(kept[1::2]), "row", perm)
                if bit == 1:
                    first.append(got)
                kept = [
                    mine + got[at * tile_rows : (at + 1) * tile_rows]
                    for at, mine in enumerate(kept[0::2])
                ]
                bit *= 2
            done.append(kept[0])
        return jnp.concatenate(done, axis=1), tuple(first)

    late_part = applied(late_slots, inverse_late, tdot(diag_inv[1], rhs[1]))
    late_block, late_first = scatter_rows(late_part)
    carried = sum(
        dot(
            lax.dynamic_slice_in_dim(coupling, tile_row[r] * tile_rows, tile_rows, axis=1),
            inverse_early[r * tile_rows : (r + 1) * tile_rows],
        )
        for r in range(row_count)
    )
    own_early = tdot(diag_inv[0], rhs[0])
    early_part = applied(early_slots, inverse_early, own_early, (late_part,), late_first)
    early_block, _ = scatter_rows(early_part - tdot(carried, late_block))
    adjoint = jnp.stack([early_block, late_block])

    scaled_z = jnp.repeat(cand_z * inv_scale[:, None], task_count, axis=1)
    query_onehot = (cand_task[:, None] == jnp.arange(task_count)[None, :]).astype(jnp.float32)
    group = jnp.arange(adj_width)[:, None] // task_count == jnp.arange(cand_z.shape[1])[None, :]
    group = group.astype(jnp.float32)
    cov_rows = dot(task_cov, query_onehot.T)

    def gradients(index, block):
        points = train_x[:, index, :]
        scaled_x = points * inv_scale[:, None]
        distance = jnp.sum(jnp.square(scaled_x[:, :, None] - scaled_z[:, None, :]), axis=0)
        kernel_vals = jnp.exp(-0.5 * distance)
        task = train_task[index]
        point_onehot = (jnp.arange(task_count)[:, None] == task[None, :]).astype(jnp.float32)
        weighted = block * kernel_vals
        pulled = weighted * tdot(point_onehot, cov_rows)
        by_task = dot(point_onehot, weighted)
        moments = dot(jnp.concatenate([points, jnp.ones_like(points[:1])]), pulled)
        return by_task, moments

    late_task, late_moment = gradients(1, late_block)
    early_task, early_moment = gradients(0, early_block)
    cov_part = dot(late_task + early_task, query_onehot)
    moments = dot(late_moment + early_moment, group)
    moments, cov_total = small_sums(moments, cov_part, row_count, col_count)
    moment, totals = moments[:-1], moments[-1]
    grad_cov = cov_total * (task_count / math.sqrt(2 * block_rows * adj_width * col_count))
    grad_z = (
        jnp.square(inv_scale)[:, None]
        * (moment - cand_z * totals[None, :])
        * (16.0 / math.sqrt(2 * block_rows))
    )
    return (adjoint, grad_z, grad_cov)


def solution(mesh):
    placed = (
        P("row", None, "col"),
        P("row", "col"),
        P(None, "row", "col"),
        P("row", None),
        P(None, "row", None),
        P(),
        P(None, None, "row"),
        P(None, "row"),
        P(None, "col"),
        P("col"),
        P(),
        P(),
    )
    return jax.shard_map(
        per_device,
        mesh=mesh,
        in_specs=placed,
        out_specs=(P(None, "row", "col"), P(None, "col"), P()),
        check_vma=False,
    )
```

```python
import functools
import math

import jax
import jax.numpy as jnp
from jax import lax
from jax.experimental import pallas as pl
from jax.experimental.pallas import tpu as pltpu
from jax.sharding import PartitionSpec as P

SPLIT = lax.Precision.HIGH
MESH = pl.DeviceIdType.MESH


def tdot(left, right):
    return lax.dot_general(left, right, (((0,), (0,)), ((), ())), precision=SPLIT)


def halves(value):
    high = lax.reduce_precision(value, 8, 7)
    return jnp.concatenate(
        [high.astype(jnp.bfloat16), (value - high).astype(jnp.bfloat16)], axis=1
    )


def halves_tdot(left, right):
    both = lax.dot_general(
        left, right, (((0,), (0,)), ((), ())), preferred_element_type=jnp.float32
    )
    rows, columns = left.shape[1] // 2, right.shape[1] // 2
    cross = both[rows:, :columns] + both[:rows, columns:]
    return both[:rows, :columns] + cross


def dot(left, right):
    return jnp.dot(left, right, precision=SPLIT)


def sums_kernel(row_count, col_count, top, x_ref, out_ref, rbuf, cbuf, rsend, rrecv, csend, crecv):
    me_row, me_col = lax.axis_index("row"), lax.axis_index("col")
    barrier = pltpu.get_barrier_semaphore()
    for j in range(1, row_count):
        pl.semaphore_signal(barrier, inc=1, device_id={"row": me_row ^ j}, device_id_type=MESH)
    for j in range(1, col_count):
        pl.semaphore_signal(barrier, inc=1, device_id={"col": me_col ^ j}, device_id_type=MESH)
    pl.semaphore_wait(barrier, row_count + col_count - 2)

    def exchange(axis, me, count, source, buffer, send, recv):
        copies = []
        for j in range(1, count):
            copy = pltpu.make_async_remote_copy(
                src_ref=source,
                dst_ref=buffer.at[me],
                send_sem=send.at[j],
                recv_sem=recv.at[j],
                device_id={axis: me ^ j},
                device_id_type=MESH,
            )
            copy.start()
            copies.append(copy)
        buffer[me] = source[...]
        for copy in copies:
            copy.wait()
        total = buffer[0]
        for j in range(1, count):
            total = total + buffer[j]
        return total

    out_ref[...] = exchange("row", me_row, row_count, x_ref, rbuf, rsend, rrecv)
    cov = out_ref.at[pl.ds(top, 8)]
    out_ref[pl.ds(top, 8)] = exchange("col", me_col, col_count, cov, cbuf, csend, crecv)


def small_sums(moments, cov_part, row_count, col_count):
    rows, wide = moments.shape
    tasks = cov_part.shape[0]
    top = -(-rows // 8) * 8
    packed = jnp.zeros((top + 8, 128), jnp.float32)
    packed = packed.at[:rows, :wide].set(moments).at[top : top + tasks, :tasks].set(cov_part)
    out = pl.pallas_call(
        functools.partial(sums_kernel, row_count, col_count, top),
        out_shape=jax.ShapeDtypeStruct(packed.shape, jnp.float32),
        in_specs=[pl.BlockSpec(memory_space=pltpu.VMEM)],
        out_specs=pl.BlockSpec(memory_space=pltpu.VMEM),
        scratch_shapes=[
            pltpu.VMEM((row_count,) + packed.shape, jnp.float32),
            pltpu.VMEM((col_count, 8, 128), jnp.float32),
            pltpu.SemaphoreType.DMA((row_count,)),
            pltpu.SemaphoreType.DMA((row_count,)),
            pltpu.SemaphoreType.DMA((col_count,)),
            pltpu.SemaphoreType.DMA((col_count,)),
        ],
        compiler_params=pltpu.CompilerParams(collective_id=0, has_side_effects=True),
    )(packed)
    return out[:rows, :wide], out[top : top + tasks, :tasks]


def per_device(
    panel,
    solved,
    rhs,
    coupling,
    diag_inv,
    tile_row,
    train_x,
    train_task,
    cand_z,
    cand_task,
    inv_scale,
    task_cov,
):
    row_count = lax.axis_size("row")
    col_count = lax.axis_size("col")
    outer_count = col_count // 2
    me_row = lax.axis_index("row")
    me_col = lax.axis_index("col")
    outer, inner = me_col // 2, me_col % 2
    tile_rows = rhs.shape[1]
    width = panel.shape[2]
    block_rows = tile_rows * row_count
    adj_width = solved.shape[1]
    task_count = task_cov.shape[0]

    swap = [(c, c ^ 1) for c in range(col_count)]
    ahead = [(c, c + 2) for c in range(col_count - 2)]
    back = [(c + 2, c) for c in range(col_count - 2)]

    def hop(pair):
        return lax.ppermute(pair[0], "col", ahead), lax.ppermute(pair[1], "col", back)

    def after(value, *others):
        return lax.optimization_barrier((value,) + others)[0]

    def slots(block, one, two, three):
        (r1, l1), (r2, l2), (r3, l3) = one, two, three
        first = jnp.where(outer == 0, l1, r1)
        second = jnp.where(outer <= 1, l2, r2)
        third = jnp.where(outer == 0, l3, jnp.where(outer == 3, r3, l1))
        return [block, first, second, third]

    def whole(block):
        groups = [[o * 2 + i for o in range(outer_count)] for i in range(2)]
        return lax.all_gather(block, "col", axis_index_groups=groups, axis=1, tiled=True)

    per_tile = tile_rows // width
    stored_of = jnp.argsort(tile_row)
    chained = outer_count == 4 and per_tile == 2

    panel_late = panel[:, 1, :]
    panel_early = panel[:, 0, :]
    other_solved = lax.ppermute(solved, "col", swap)
    if chained:
        late1 = hop((panel_late, panel_late))
        early1 = hop((panel_early, panel_early))
        late2 = hop(late1)
        early2 = hop(early1)
        late3 = hop(late2)
        early3 = hop(early2)
        sources = [
            outer,
            jnp.where(outer == 0, 1, outer - 1),
            jnp.where(outer <= 1, outer + 2, outer - 2),
            jnp.where(outer == 0, 3, jnp.where(outer == 3, 0, outer + 1)),
        ]
    else:
        late_slots, early_slots = [whole(panel_late)], [whole(panel_early)]
    inverse_early = lax.all_gather(diag_inv[0], "row", axis=0, tiled=True)
    inverse_late = lax.all_gather(
        after(diag_inv[1], inverse_early), "row", axis=0, tiled=True
    )
    own_halves, other_halves = halves(solved), halves(other_solved)
    own_late, own_early = tdot(diag_inv[1], rhs[1]), tdot(diag_inv[0], rhs[0])
    carried = sum(
        dot(
            lax.dynamic_slice_in_dim(coupling, tile_row[r] * tile_rows, tile_rows, axis=1),
            inverse_early[r * tile_rows : (r + 1) * tile_rows],
        )
        for r in range(row_count)
    )

    def products(block):
        parts = halves(block)
        return halves_tdot(parts, own_halves), halves_tdot(parts, other_halves)

    if chained:
        ready = [
            products(slot)
            for block, one in ((panel_late, late1), (panel_early, early1))
            for slot in (block, jnp.where(outer == 0, one[1], one[0]))
        ]
        late3, ready, own_late, own_early, carried = lax.optimization_barrier(
            (late3, ready, own_late, own_early, carried)
        )
        late_slots = ready[:2] + slots(panel_late, late1, late2, late3)[2:]
        early_slots = ready[2:] + slots(panel_early, early1, early2, early3)[2:]

    def rows_of(matrix, tile):
        return lax.dynamic_slice_in_dim(matrix, tile * tile_rows, tile_rows, axis=0)

    def swapped(block):
        own, sent = block if isinstance(block, tuple) else products(block)
        return own, lax.ppermute(sent, "col", swap)

    def applied(blocks, inverse, total, before=(), beside=()):
        if chained:
            for at, (block, source) in enumerate(zip(blocks, sources)):
                if at == len(blocks) - 1:
                    block, total = lax.optimization_barrier((block, total) + before)[:2]
                own, got = swapped(block)
                if at == len(blocks) - 1:
                    got = after(got, *beside)
                update = jnp.concatenate(
                    [jnp.where(inner == 0, own, got), jnp.where(inner == 0, got, own)]
                )
                total = total - tdot(rows_of(inverse, stored_of[source]), update)
            return total
        own, got = swapped(blocks[0])
        ids = jnp.arange(outer_count) * 2
        pieces = jnp.concatenate([ids + inner, ids + 1 - inner])
        position = stored_of[pieces // per_tile] * per_tile + pieces % per_tile
        update = jnp.concatenate([own, got]).reshape(-1, width, adj_width)
        update = jnp.take(update, jnp.argsort(position), axis=0, mode="clip")
        return total - tdot(inverse, update.reshape(block_rows, adj_width))

    def scatter_rows(partial_value):
        done, first = [], []
        cut = 2 if adj_width % 256 == 0 else 1
        for part in jnp.split(partial_value, cut, axis=1):
            kept = [rows_of(part, tile_row[me_row ^ j]) for j in range(row_count)]
            bit = 1
            while bit < row_count:
                perm = [(r, r ^ bit) for r in range(row_count)]
                got = lax.ppermute(jnp.concatenate(kept[1::2]), "row", perm)
                if bit == 1:
                    first.append(got)
                kept = [
                    mine + got[at * tile_rows : (at + 1) * tile_rows]
                    for at, mine in enumerate(kept[0::2])
                ]
                bit *= 2
            done.append(kept[0])
        return jnp.concatenate(done, axis=1), tuple(first)

    late_part = applied(late_slots, inverse_late, own_late)
    late_block, late_first = scatter_rows(late_part)
    early_part = applied(early_slots, inverse_early, own_early, (late_part,), late_first)
    early_block, _ = scatter_rows(early_part - tdot(carried, late_block))
    adjoint = jnp.stack([early_block, late_block])

    scaled_z = jnp.repeat(cand_z * inv_scale[:, None], task_count, axis=1)
    query_onehot = (cand_task[:, None] == jnp.arange(task_count)[None, :]).astype(jnp.float32)
    group = jnp.arange(adj_width)[:, None] // task_count == jnp.arange(cand_z.shape[1])[None, :]
    group = group.astype(jnp.float32)
    cov_rows = dot(task_cov, query_onehot.T)

    def gradients(index, block):
        points = train_x[:, index, :]
        scaled_x = points * inv_scale[:, None]
        distance = jnp.sum(jnp.square(scaled_x[:, :, None] - scaled_z[:, None, :]), axis=0)
        kernel_vals = jnp.exp(-0.5 * distance)
        task = train_task[index]
        point_onehot = (jnp.arange(task_count)[:, None] == task[None, :]).astype(jnp.float32)
        weighted = block * kernel_vals
        pulled = weighted * tdot(point_onehot, cov_rows)
        by_task = dot(point_onehot, weighted)
        moments = dot(jnp.concatenate([points, jnp.ones_like(points[:1])]), pulled)
        return by_task, moments

    late_task, late_moment = gradients(1, late_block)
    early_task, early_moment = gradients(0, early_block)
    cov_part = dot(late_task + early_task, query_onehot)
    moments = dot(late_moment + early_moment, group)
    moments, cov_total = small_sums(moments, cov_part, row_count, col_count)
    moment, totals = moments[:-1], moments[-1]
    grad_cov = cov_total * (task_count / math.sqrt(2 * block_rows * adj_width * col_count))
    grad_z = (
        jnp.square(inv_scale)[:, None]
        * (moment - cand_z * totals[None, :])
        * (16.0 / math.sqrt(2 * block_rows))
    )
    return (adjoint, grad_z, grad_cov)


def solution(mesh):
    placed = (
        P("row", None, "col"),
        P("row", "col"),
        P(None, "row", "col"),
        P("row", None),
        P(None, "row", None),
        P(),
        P(None, None, "row"),
        P(None, "row"),
        P(None, "col"),
        P("col"),
        P(),
        P(),
    )
    return jax.shard_map(
        per_device,
        mesh=mesh,
        in_specs=placed,
        out_specs=(P(None, "row", "col"), P(None, "col"), P()),
        check_vma=False,
    )
```

```python
import functools
import math

import jax
import jax.numpy as jnp
from jax import lax
from jax.experimental import pallas as pl
from jax.experimental.pallas import tpu as pltpu
from jax.sharding import PartitionSpec as P

SPLIT = lax.Precision.HIGH
MESH = pl.DeviceIdType.MESH


def tdot(left, right):
    return lax.dot_general(left, right, (((0,), (0,)), ((), ())), precision=SPLIT)


def halves(value):
    high = lax.reduce_precision(value, 8, 7)
    return jnp.concatenate(
        [high.astype(jnp.bfloat16), (value - high).astype(jnp.bfloat16)], axis=1
    )


def halves_tdot(left, right):
    both = lax.dot_general(
        left, right, (((0,), (0,)), ((), ())), preferred_element_type=jnp.float32
    )
    rows, columns = left.shape[1] // 2, right.shape[1] // 2
    cross = both[rows:, :columns] + both[:rows, columns:]
    return both[:rows, :columns] + cross


def dot(left, right):
    return jnp.dot(left, right, precision=SPLIT)


def sums_kernel(row_count, col_count, top, x_ref, out_ref, rbuf, cbuf, rsend, rrecv, csend, crecv):
    me_row, me_col = lax.axis_index("row"), lax.axis_index("col")
    barrier = pltpu.get_barrier_semaphore()
    for j in range(1, row_count):
        pl.semaphore_signal(barrier, inc=1, device_id={"row": me_row ^ j}, device_id_type=MESH)
    for j in range(1, col_count):
        pl.semaphore_signal(barrier, inc=1, device_id={"col": me_col ^ j}, device_id_type=MESH)
    pl.semaphore_wait(barrier, row_count + col_count - 2)

    def exchange(axis, me, count, source, buffer, send, recv):
        copies = []
        for j in range(1, count):
            copy = pltpu.make_async_remote_copy(
                src_ref=source,
                dst_ref=buffer.at[me],
                send_sem=send.at[j],
                recv_sem=recv.at[j],
                device_id={axis: me ^ j},
                device_id_type=MESH,
            )
            copy.start()
            copies.append(copy)
        buffer[me] = source[...]
        for copy in copies:
            copy.wait()
        total = buffer[0]
        for j in range(1, count):
            total = total + buffer[j]
        return total

    out_ref[...] = exchange("row", me_row, row_count, x_ref, rbuf, rsend, rrecv)
    cov = out_ref.at[pl.ds(top, 8)]
    out_ref[pl.ds(top, 8)] = exchange("col", me_col, col_count, cov, cbuf, csend, crecv)


def small_sums(moments, cov_part, row_count, col_count):
    rows, wide = moments.shape
    tasks = cov_part.shape[0]
    top = -(-rows // 8) * 8
    packed = jnp.zeros((top + 8, 128), jnp.float32)
    packed = packed.at[:rows, :wide].set(moments).at[top : top + tasks, :tasks].set(cov_part)
    out = pl.pallas_call(
        functools.partial(sums_kernel, row_count, col_count, top),
        out_shape=jax.ShapeDtypeStruct(packed.shape, jnp.float32),
        in_specs=[pl.BlockSpec(memory_space=pltpu.VMEM)],
        out_specs=pl.BlockSpec(memory_space=pltpu.VMEM),
        scratch_shapes=[
            pltpu.VMEM((row_count,) + packed.shape, jnp.float32),
            pltpu.VMEM((col_count, 8, 128), jnp.float32),
            pltpu.SemaphoreType.DMA((row_count,)),
            pltpu.SemaphoreType.DMA((row_count,)),
            pltpu.SemaphoreType.DMA((col_count,)),
            pltpu.SemaphoreType.DMA((col_count,)),
        ],
        compiler_params=pltpu.CompilerParams(collective_id=0, has_side_effects=True),
    )(packed)
    return out[:rows, :wide], out[top : top + tasks, :tasks]


def per_device(
    panel,
    solved,
    rhs,
    coupling,
    diag_inv,
    tile_row,
    train_x,
    train_task,
    cand_z,
    cand_task,
    inv_scale,
    task_cov,
):
    row_count = lax.axis_size("row")
    col_count = lax.axis_size("col")
    outer_count = col_count // 2
    me_row = lax.axis_index("row")
    me_col = lax.axis_index("col")
    outer, inner = me_col // 2, me_col % 2
    tile_rows = rhs.shape[1]
    width = panel.shape[2]
    block_rows = tile_rows * row_count
    adj_width = solved.shape[1]
    task_count = task_cov.shape[0]

    swap = [(c, c ^ 1) for c in range(col_count)]
    ahead = [(c, c + 2) for c in range(col_count - 2)]
    back = [(c + 2, c) for c in range(col_count - 2)]

    def hop(pair):
        return lax.ppermute(pair[0], "col", ahead), lax.ppermute(pair[1], "col", back)

    def after(value, *others):
        return lax.optimization_barrier((value,) + others)[0]

    def slots(block, one, two, three):
        (r1, l1), (r2, l2), (r3, l3) = one, two, three
        first = jnp.where(outer == 0, l1, r1)
        second = jnp.where(outer <= 1, l2, r2)
        third = jnp.where(outer == 0, l3, jnp.where(outer == 3, r3, l1))
        return [block, first, second, third]

    def whole(block):
        groups = [[o * 2 + i for o in range(outer_count)] for i in range(2)]
        return lax.all_gather(block, "col", axis_index_groups=groups, axis=1, tiled=True)

    per_tile = tile_rows // width
    stored_of = jnp.argsort(tile_row)
    chained = outer_count == 4 and per_tile == 2

    panel_late = panel[:, 1, :]
    panel_early = panel[:, 0, :]
    other_solved = lax.ppermute(solved, "col", swap)
    inverse_early = lax.all_gather(diag_inv[0], "row", axis=0, tiled=True)
    own_late, own_early = tdot(diag_inv[1], rhs[1]), tdot(diag_inv[0], rhs[0])
    carried = sum(
        dot(
            lax.dynamic_slice_in_dim(coupling, tile_row[r] * tile_rows, tile_rows, axis=1),
            inverse_early[r * tile_rows : (r + 1) * tile_rows],
        )
        for r in range(row_count)
    )
    if chained:
        late1 = hop((panel_late, panel_late))
        early1 = hop((panel_early, panel_early))
        late2 = hop(late1)
        early2 = hop(early1)
        late2, own_late, own_early = lax.optimization_barrier((late2, own_late, own_early))
        late3 = hop(late2)
        early2, other_solved, carried = lax.optimization_barrier((early2, other_solved, carried))
        early3 = hop(early2)
        late_slots = slots(panel_late, late1, late2, late3)
        early_slots = slots(panel_early, early1, early2, early3)
        sources = [
            outer,
            jnp.where(outer == 0, 1, outer - 1),
            jnp.where(outer <= 1, outer + 2, outer - 2),
            jnp.where(outer == 0, 3, jnp.where(outer == 3, 0, outer + 1)),
        ]
    else:
        late_slots, early_slots = [whole(panel_late)], [whole(panel_early)]
    inverse_late = lax.all_gather(
        after(diag_inv[1], inverse_early), "row", axis=0, tiled=True
    )
    own_halves, other_halves = halves(solved), halves(other_solved)

    def rows_of(matrix, tile):
        return lax.dynamic_slice_in_dim(matrix, tile * tile_rows, tile_rows, axis=0)

    def swapped(block):
        parts = halves(block)
        sent = halves_tdot(parts, other_halves)
        return halves_tdot(parts, own_halves), lax.ppermute(sent, "col", swap)

    def applied(blocks, inverse, total, before=(), beside=()):
        if chained:
            for at, (block, source) in enumerate(zip(blocks, sources)):
                if at == len(blocks) - 1:
                    block, total = lax.optimization_barrier((block, total) + before)[:2]
                own, got = swapped(block)
                if at == len(blocks) - 1:
                    got = after(got, *beside)
                update = jnp.concatenate(
                    [jnp.where(inner == 0, own, got), jnp.where(inner == 0, got, own)]
                )
                total = total - tdot(rows_of(inverse, stored_of[source]), update)
            return total
        own, got = swapped(blocks[0])
        ids = jnp.arange(outer_count) * 2
        pieces = jnp.concatenate([ids + inner, ids + 1 - inner])
        position = stored_of[pieces // per_tile] * per_tile + pieces % per_tile
        update = jnp.concatenate([own, got]).reshape(-1, width, adj_width)
        update = jnp.take(update, jnp.argsort(position), axis=0, mode="clip")
        return total - tdot(inverse, update.reshape(block_rows, adj_width))

    def scatter_rows(partial_value):
        done, first = [], []
        cut = 2 if adj_width % 256 == 0 else 1
        for part in jnp.split(partial_value, cut, axis=1):
            kept = [rows_of(part, tile_row[me_row ^ j]) for j in range(row_count)]
            bit = 1
            while bit < row_count:
                perm = [(r, r ^ bit) for r in range(row_count)]
                got = lax.ppermute(jnp.concatenate(kept[1::2]), "row", perm)
                if bit == 1:
                    first.append(got)
                kept = [
                    mine + got[at * tile_rows : (at + 1) * tile_rows]
                    for at, mine in enumerate(kept[0::2])
                ]
                bit *= 2
            done.append(kept[0])
        return jnp.concatenate(done, axis=1), tuple(first)

    late_part = applied(late_slots, inverse_late, own_late)
    late_block, late_first = scatter_rows(late_part)
    early_part = applied(early_slots, inverse_early, own_early, (late_part,), late_first)
    early_block, _ = scatter_rows(early_part - tdot(carried, late_block))
    adjoint = jnp.stack([early_block, late_block])

    scaled_z = jnp.repeat(cand_z * inv_scale[:, None], task_count, axis=1)
    query_onehot = (cand_task[:, None] == jnp.arange(task_count)[None, :]).astype(jnp.float32)
    group = jnp.arange(adj_width)[:, None] // task_count == jnp.arange(cand_z.shape[1])[None, :]
    group = group.astype(jnp.float32)
    cov_rows = dot(task_cov, query_onehot.T)

    def gradients(index, block):
        points = train_x[:, index, :]
        scaled_x = points * inv_scale[:, None]
        distance = jnp.sum(jnp.square(scaled_x[:, :, None] - scaled_z[:, None, :]), axis=0)
        kernel_vals = jnp.exp(-0.5 * distance)
        task = train_task[index]
        point_onehot = (jnp.arange(task_count)[:, None] == task[None, :]).astype(jnp.float32)
        weighted = block * kernel_vals
        pulled = weighted * tdot(point_onehot, cov_rows)
        by_task = dot(point_onehot, weighted)
        moments = dot(jnp.concatenate([points, jnp.ones_like(points[:1])]), pulled)
        return by_task, moments

    late_task, late_moment = gradients(1, late_block)
    early_task, early_moment = gradients(0, early_block)
    cov_part = dot(late_task + early_task, query_onehot)
    moments = dot(late_moment + early_moment, group)
    moments, cov_total = small_sums(moments, cov_part, row_count, col_count)
    moment, totals = moments[:-1], moments[-1]
    grad_cov = cov_total * (task_count / math.sqrt(2 * block_rows * adj_width * col_count))
    grad_z = (
        jnp.square(inv_scale)[:, None]
        * (moment - cand_z * totals[None, :])
        * (16.0 / math.sqrt(2 * block_rows))
    )
    return (adjoint, grad_z, grad_cov)


def solution(mesh):
    placed = (
        P("row", None, "col"),
        P("row", "col"),
        P(None, "row", "col"),
        P("row", None),
        P(None, "row", None),
        P(),
        P(None, None, "row"),
        P(None, "row"),
        P(None, "col"),
        P("col"),
        P(),
        P(),
    )
    return jax.shard_map(
        per_device,
        mesh=mesh,
        in_specs=placed,
        out_specs=(P(None, "row", "col"), P(None, "col"), P()),
        check_vma=False,
    )
```
